1024 devices in a mesh: ctx: 8 (over y, core), head: 16 (over z_lo), wide: 8 (over z_hi, x).
Axes of the slice: x: 4, y: 4, z: 32 (z_hi: 2, z_lo: 16; z = z_hi * 16 + z_lo), core: 2. Of those that a mesh axis runs over, the one named last changes fastest.
Arguments:
- query_rows: bfloat16 [8, 2048, 4096], P('wide', 'ctx', 'head'), may hold values from -105 to 105
- key_rows: bfloat16 [8, 2048, 4096], P('wide', 'ctx', 'head'), may hold values from -4.5 to 4.5
- value_rows: bfloat16 [8, 2048, 4096], P('wide', 'ctx', 'head'), may hold values from -6 to 6
- grad_out: bfloat16 [8, 2048, 4096], P('wide', 'ctx', 'head'), may hold values from -6 to 6
- segment: int32 [8, 2048], P('wide', 'ctx'), may hold values from 0 to 15, never falling along the last dimension, each value on 1 to 256 neighbouring positions
- frames: bfloat16 [8, 2048, 4096], P(None, 'ctx', 'wide'), may hold values from -6 to 6
Outputs:
- grad_query: bfloat16 [8, 2048, 4096], P('wide', 'ctx', 'head')
- grad_key: bfloat16 [8, 2048, 4096], P('wide', 'ctx', 'head')
- grad_value: bfloat16 [8, 2048, 4096], P('wide', 'ctx', 'head')
- grad_wq: float32 [8, 512, 4096], P('wide', 'ctx', 'head')
The draws below stay inside these ranges and needn't reach their ends.
Inputs may be any that keep to these rules, and one draw needn't show every extreme that they name: Ids never fall along a recording; each segment spans 1 to 256 frames and one spans exactly 256.
All inputs are finite; a program needn't handle non-finite values.
Results may differ from the reference program's by a relative error of at most 0.01.
Values may be sent and summed in bfloat16 or wider, within the bound.
A program may use at most 32 MiB of HBM per device.

```python
import math
import jax
import jax.numpy as jnp
import numpy as np
from jax import lax

D = 4096
HD = 128
TOK = 256
HEADS = 32
HQ = 4096
SEQ = 2048
RECS = 8
SEGMENTS = 16
N_WIDE = 8


def base_keys(key):
    return jnp.clip(jax.random.normal(jax.random.fold_in(key, 101), (RECS, SEQ, HQ), jnp.float32), -4.0, 4.0)


def draw_key_rows(key, part):
    base = base_keys(key)
    return base.astype(jnp.bfloat16)


def draw_query_rows(key, part):
    fresh = jnp.clip(jax.random.normal(jax.random.fold_in(key, 103), (RECS, SEQ, HQ), jnp.float32), -4.0, 4.0)
    return fresh.astype(jnp.bfloat16)


def with_spikes(values, key, source, target, shards_of, factor):
    def block_of(position):
        return (jnp.arange(values.shape[position]) // (values.shape[position] // shards_of)).reshape((-1,) + (1,) * (values.ndim - 1 - position))

    one_side = jax.random.permutation(key, shards_of)[block_of(target)]
    far = (block_of(target) + shards_of // 2) % shards_of
    return jnp.where((block_of(source) == one_side) | (block_of(source) == far), factor * values, values)


def level_of(key, shape, shards, least, largest):
    gain = 1.0
    for position, shards_of in shards:
        draws = jax.random.uniform(jax.random.fold_in(jax.random.fold_in(key, 6), position), (shards_of,), jnp.float32, least / len(shards), largest / len(shards))
        gain = gain * jnp.repeat(jnp.exp(draws), shape[position] // shards_of).reshape((-1,) + (1,) * (len(shape) - 1 - position))
    return gain


def profile(number_of, total, most, lean):
    weights = [(1 << 20) // math.isqrt(rank ** lean) + 1 for rank in range(2, number_of + 1)]
    rest, holding = total - most - (number_of - 1), [1] * (number_of - 1)
    while rest > 0:
        movable = [i for i in range(number_of - 1) if holding[i] < most]
        whole, budget = sum([weights[i] for i in movable]), rest
        for i in movable:
            addition = min(most - holding[i], max(1, budget * weights[i] // whole), rest)
            holding[i] = holding[i] + addition
            rest = rest - addition
    return np.array([most] + holding)


def uneven(stream_key, number_of, total, limit, lean):
    if number_of == 2:
        one = jax.random.randint(stream_key, (), max(1, total - limit), min(limit, total - 1) + 1)
        return jnp.stack([one, total - one])
    lengths = jnp.asarray(profile(number_of, total, limit, lean), jnp.int32)
    pairs = (number_of - 1) // 2
    donor, taker = lengths[1:1 + 2 * pairs:2], lengths[2:2 + 2 * pairs:2]
    margin = jnp.minimum(donor - 1, limit - taker)
    moved = jax.random.randint(jax.random.fold_in(stream_key, 1), (pairs,), 0, 1 << 20) % (margin + 1)
    lengths = lengths.at[1:1 + 2 * pairs:2].set(donor - moved).at[2:2 + 2 * pairs:2].set(taker + moved)
    return lengths[jax.random.permutation(jax.random.fold_in(stream_key, 2), number_of)]


def gaussian(key, extent, deviation, bound, shards=(), held_as=jnp.bfloat16):
    drawn = deviation * jax.random.normal(key, extent, jnp.float32)
    if shards:
        drawn = drawn * level_of(key, extent, shards, -0.22, 0.18)
    return jnp.clip(drawn, -bound, bound).astype(held_as)


def heavy_noise(key, extent, spread, bound, pieces, heavy, held_as=jnp.bfloat16):
    values = spread * jax.random.normal(key, extent, jnp.float32)
    if pieces:
        values = values * level_of(key, extent, pieces, -0.22, 0.18)
    return jnp.clip(with_spikes(values, jax.random.fold_in(key, 3), *heavy), -bound, bound).astype(held_as)


def setup_inputs(seed: int = 0) -> dict:
    splits = jax.random.split(jax.random.key(seed), 7)
    return {
        "query_rows": draw_query_rows(jax.random.fold_in(splits[6], 71), 0),
        "key_rows": draw_key_rows(jax.random.fold_in(splits[6], 71), 0),
        "value_rows": gaussian(splits[2], (RECS, SEQ, HQ), 1.0, 6.0, ((0, 8), (1, 8), (2, 16))),
        "grad_out": gaussian(splits[3], (RECS, SEQ, HQ), 1.0, 6.0, ((0, 8), (1, 8), (2, 16))),
        "segment": jax.vmap(lambda own: jnp.searchsorted(jnp.cumsum(uneven(own, SEGMENTS, SEQ, TOK, 1)), jnp.arange(SEQ), side="right"))(jax.random.split(splits[4], RECS)).reshape((RECS, SEQ)).astype(jnp.int32),
        "frames": heavy_noise(splits[5], (RECS, SEQ, D), 1.0, 6.0, ((1, 8), (2, 8)), (1, 2, 8, 2.0)),
    }


def windows(blocks, filler):
    earlier = jnp.concatenate([filler, blocks[:-1]], axis=0)
    return jnp.concatenate([earlier, blocks], axis=1)


def head_grads(inputs):
    query_head, key_head, value_head, grad_head, segment_head = inputs
    blocks = SEQ // TOK
    factor = HD ** -0.5
    query_block = query_head.reshape(blocks, TOK, HD).astype(jnp.float32)
    grad_block = grad_head.reshape(blocks, TOK, HD).astype(jnp.float32)
    key_window = windows(key_head.reshape(blocks, TOK, HD), jnp.zeros((1, TOK, HD), key_head.dtype)).astype(jnp.float32)
    value_window = windows(value_head.reshape(blocks, TOK, HD), jnp.zeros((1, TOK, HD), value_head.dtype)).astype(jnp.float32)
    segment_block = segment_head.reshape(blocks, TOK)
    segment_window = windows(segment_block, jnp.full((1, TOK), -1, jnp.int32))
    places = jnp.arange(TOK, dtype=jnp.int32)
    key_places = jnp.concatenate([places - TOK, places])
    allowed = (segment_block[:, :, None] == segment_window[:, None, :]) & (key_places[None, None, :] <= places[None, :, None])
    scores = jnp.einsum("bid,bjd->bij", query_block, key_window) * factor
    row_max = jnp.max(jnp.where(allowed, scores, -jnp.inf), axis=2, keepdims=True)
    row_total = jnp.sum(jnp.where(allowed, jnp.exp(scores - row_max), 0.0), axis=2, keepdims=True)
    log_total = row_max + jnp.log(row_total)
    prob = jnp.where(allowed, jnp.exp(scores - log_total), 0.0)
    prob_low = prob.astype(jnp.bfloat16)
    grad_prob = jnp.einsum("bid,bjd->bij", grad_block, value_window)
    row_delta = jnp.sum(prob * grad_prob, axis=2, keepdims=True)
    grad_score = (prob * (grad_prob - row_delta)).astype(jnp.bfloat16).astype(jnp.float32)
    grad_query = (jnp.einsum("bij,bjd->bid", grad_score, key_window) * factor).astype(jnp.bfloat16)
    key_window_grad = jnp.einsum("bij,bid->bjd", grad_score, query_block)
    value_window_grad = jnp.einsum("bij,bid->bjd", prob_low.astype(jnp.float32), grad_block)
    zero_block = jnp.zeros((1, TOK, HD), jnp.float32)
    key_grad = (key_window_grad[:, TOK:] + jnp.concatenate([key_window_grad[1:, :TOK], zero_block], axis=0)) * factor
    value_grad = value_window_grad[:, TOK:] + jnp.concatenate([value_window_grad[1:, :TOK], zero_block], axis=0)
    return (grad_query.reshape(SEQ, HD), key_grad.astype(jnp.bfloat16).reshape(SEQ, HD),
            value_grad.astype(jnp.bfloat16).reshape(SEQ, HD))


def to_heads(array):
    return array.reshape(RECS, SEQ, HEADS, HD).transpose(0, 2, 1, 3).reshape(RECS * HEADS, SEQ, HD)


def from_heads(array):
    return array.reshape(RECS, HEADS, SEQ, HD).transpose(0, 2, 1, 3).reshape(RECS, SEQ, HEADS * HD)


def reference(query_rows, key_rows, value_rows, grad_out, segment, frames):
    segment_all = jnp.repeat(segment, HEADS, axis=0)
    grad_query, grad_key, grad_value = lax.map(head_grads, (to_heads(query_rows), to_heads(key_rows), to_heads(value_rows), to_heads(grad_out), segment_all))
    grad_query = from_heads(grad_query)
    grad_wq = jnp.dot(frames.reshape(RECS * SEQ, D).T, grad_query.reshape(RECS * SEQ, HQ), preferred_element_type=jnp.float32)
    return grad_query, from_heads(grad_key), from_heads(grad_value), grad_wq.reshape(N_WIDE, D // N_WIDE, HQ)
```

```python
import functools

import jax
import jax.numpy as jnp
from jax import lax
from jax.experimental import pallas as pl
from jax.experimental.pallas import tpu as pltpu
from jax.sharding import PartitionSpec as P

HD = 128
MESH = pl.DeviceIdType.MESH
F32 = jnp.float32
BF16 = jnp.bfloat16
LOW = -1e30


def dot(a, b, dims):
    return lax.dot_general(a, b, (dims, ((), ())), preferred_element_type=F32)


def remote(src, dst, send, recv, where):
    return pltpu.make_async_remote_copy(
        src_ref=src, dst_ref=dst, send_sem=send, recv_sem=recv, device_id=where, device_id_type=MESH
    )


def kernel(
    nc, nx, heads, tok, width, parts,
    q_in, k_in, v_in, g_in, seg_in, fr_in,
    gq_out, gk_out, gv_out, wq_out,
    q, k, v, g, seg, bias, fl, ff, flt, fft, sc, dp, dsb, pb,
    lbuf, fbuf, acc, rs_s, rs_r, gqb, gkb, gvb, pks, pvs, pkr, pvr, wqb,
    in_sem, fl_sem, ff_sem, out_sem, kv_s, kv_r, pp_s, pp_r, z_s, z_r, xl_s, xl_r, xf_s, xf_r, c_s, c_r,
):
    c = lax.axis_index("ctx")
    w = lax.axis_index("wide")
    x = lax.rem(w, nx)
    half = w // nx
    part = tok // parts
    rows = width // nc
    factor = HD ** (-0.5)

    def ctx(step):
        return {"ctx": lax.rem(c + step, nc)}

    def across(step):
        return {"wide": half * nx + lax.rem(x + step, nx)}

    partner = {"wide": lax.rem(w + nx, 2 * nx)}

    barrier = pltpu.get_barrier_semaphore()
    others = [partner] + [across(j) for j in range(1, nx)] + [ctx(j) for j in range(1, nc)]
    for other in others:
        pl.semaphore_signal(barrier, inc=1, device_id=other, device_id_type=MESH)

    loads = []
    for h in range(heads):
        cols = pl.ds(h * HD, HD)
        loads.append(pltpu.make_async_copy(q_in.at[0, :, cols], q.at[h], in_sem.at[4 * h]))
        loads.append(pltpu.make_async_copy(k_in.at[0, :, cols], k.at[h, pl.ds(tok, tok)], in_sem.at[4 * h + 1]))
        loads.append(pltpu.make_async_copy(g_in.at[0, :, cols], g.at[h], in_sem.at[4 * h + 2]))
        loads.append(pltpu.make_async_copy(v_in.at[0, :, cols], v.at[h, pl.ds(tok, tok)], in_sem.at[4 * h + 3]))
    loads.append(pltpu.make_async_copy(seg_in, seg.at[1], in_sem.at[4 * heads]))
    own_frames = pltpu.make_async_copy(fr_in.at[pl.ds(half * nx, nx)], fl, fl_sem)
    far_frames = [
        pltpu.make_async_copy(
            fr_in.at[(1 - half) * nx + r, pl.ds(i * part, part)], ff.at[i, r], ff_sem.at[i * nx + r]
        )
        for i in range(parts)
        for r in range(nx)
    ]
    for copy in loads + [own_frames] + far_frames:
        copy.start()
    for copy in loads:
        copy.wait()

    for h in range(heads):
        sc[h, :, tok:] = dot(q[h], k[h, tok:], ((1,), (1,))) * factor
        dp[h, :, tok:] = dot(g[h], v[h, tok:], ((1,), (1,)))

    own_frames.wait()
    for r in range(nx):
        flt[r] = fl[r].T
    for copy in far_frames:
        copy.wait()
    for i in range(parts):
        fft[i] = ff[i].reshape(nx * part, width).T

    pl.semaphore_wait(barrier, len(others))

    seg_copy = remote(seg.at[1], seg.at[0], kv_s.at[2 * heads], kv_r.at[2 * heads], ctx(1))
    seg_copy.start()
    kv = []
    for h in range(heads):
        for n, ref in enumerate((k, v)):
            copy = remote(
                ref.at[h, pl.ds(tok, tok)], ref.at[h, pl.ds(0, tok)], kv_s.at[2 * h + n], kv_r.at[2 * h + n], ctx(1)
            )
            copy.start()
            kv.append(copy)

    mine = jnp.broadcast_to(seg[1], (HD, tok)).T[:, :1]
    query_place = lax.broadcasted_iota(jnp.int32, (tok, tok), 0)
    key_place = lax.broadcasted_iota(jnp.int32, (tok, tok), 1)
    bias[:, tok:] = jnp.where((mine == seg[1]) & (key_place <= query_place), 0.0, LOW)
    seg_copy.wait_recv()
    bias[:, :tok] = jnp.where((mine == seg[0]) & (c > 0), 0.0, LOW)

    z_copies = {}
    xl_copies = {}
    for h in range(heads):
        kv[2 * h].wait_recv()
        sc[h, :, :tok] = dot(q[h], k[h, :tok], ((1,), (1,))) * factor
        kv[2 * h + 1].wait_recv()
        dp[h, :, :tok] = dot(g[h], v[h, :tok], ((1,), (1,)))
        scores = sc[h] + bias[...]
        row_max = jnp.max(scores, axis=1, keepdims=True)
        weight = jnp.exp(scores - row_max)
        prob = weight * (1.0 / jnp.sum(weight, axis=1, keepdims=True))
        grad_prob = dp[h]
        row_delta = jnp.sum(prob * grad_prob, axis=1, keepdims=True)
        grad_score = (prob * (grad_prob - row_delta)).astype(BF16)
        dsb[h] = grad_score
        pb[h] = prob.astype(BF16)
        grad_query = (dot(grad_score, k[h], ((1,), (0,))) * factor).astype(BF16)
        lbuf[h, x] = grad_query
        gqb[:, h * HD : (h + 1) * HD] = grad_query
        for i in range(parts):
            copy = remote(
                lbuf.at[h, x, pl.ds(i * part, part)], fbuf.at[h, i, x], z_s.at[h * parts + i], z_r.at[h * parts + i],
                partner,
            )
            copy.start()
            z_copies[h, i] = copy
        for j in range(1, nx):
            copy = remote(lbuf.at[h, x], lbuf.at[h, x], xl_s.at[h * nx + j], xl_r.at[h * nx + j], across(j))
            copy.start()
            xl_copies[h, j] = copy

    outs = [pltpu.make_async_copy(gqb, gq_out.at[0], out_sem.at[0])]
    outs[0].start()

    for h in range(heads):
        cols = slice(h * HD, (h + 1) * HD)
        pks[:, cols] = dot(dsb[h, :, :tok], q[h], ((0,), (0,)))
        pvs[:, cols] = dot(pb[h, :, :tok], g[h], ((0,), (0,)))
    pp = [
        remote(pks, pkr, pp_s.at[0], pp_r.at[0], ctx(nc - 1)),
        remote(pvs, pvr, pp_s.at[1], pp_r.at[1], ctx(nc - 1)),
    ]
    for copy in pp:
        copy.start()

    for h in range(heads):
        for j in range(1, nx):
            xl_copies[h, j].wait_recv()
        total = dot(flt[0], lbuf[h, 0], ((1,), (0,)))
        for r in range(1, nx):
            total += dot(flt[r], lbuf[h, r], ((1,), (0,)))
        acc[h] = total

    own_key = []
    for h in range(heads):
        own_key.append((dot(dsb[h, :, tok:], q[h], ((0,), (0,))), dot(pb[h, :, tok:], g[h], ((0,), (0,)))))
    for copy in pp:
        copy.wait_recv()
    for h in range(heads):
        cols = slice(h * HD, (h + 1) * HD)
        gkb[:, cols] = ((own_key[h][0] + pkr[:, cols]) * factor).astype(BF16)
        gvb[:, cols] = (own_key[h][1] + pvr[:, cols]).astype(BF16)
    outs.append(pltpu.make_async_copy(gkb, gk_out.at[0], out_sem.at[1]))
    outs.append(pltpu.make_async_copy(gvb, gv_out.at[0], out_sem.at[2]))
    outs[1].start()
    outs[2].start()

    xf_copies = {}
    c_copies = {}
    order = [(h, i) for h in range(heads) for i in range(parts)]

    def pass_on(h, i):
        z_copies[h, i].wait_recv()
        for j in range(1, nx):
            n = (h * parts + i) * nx + j
            copy = remote(fbuf.at[h, i, x], fbuf.at[h, i, x], xf_s.at[n], xf_r.at[n], across(j))
            copy.start()
            xf_copies[h, i, j] = copy

    def add(h, i):
        for j in range(1, nx):
            xf_copies[h, i, j].wait_recv()
        total = acc[h] + dot(fft[i], fbuf[h, i].reshape(nx * part, HD), ((1,), (0,)))
        acc[h] = total
        if i == parts - 1:
            rs_s[h] = total.astype(BF16).reshape(nc, rows, HD)
            for j in range(1, nc):
                to = lax.rem(c + j, nc)
                copy = remote(rs_s.at[h, to], rs_r.at[h, j], c_s.at[h * nc + j], c_r.at[h * nc + j], ctx(j))
                copy.start()
                c_copies[h, j] = copy

    pass_on(*order[0])
    for n in range(1, len(order)):
        pass_on(*order[n])
        add(*order[n - 1])
    add(*order[-1])

    for h in range(heads):
        total = acc[h, pl.ds(pl.multiple_of(c * rows, rows), rows)]
        for j in range(1, nc):
            c_copies[h, j].wait_recv()
            total += rs_r[h, j].astype(F32)
        wqb[:, h * HD : (h + 1) * HD] = total
    outs.append(pltpu.make_async_copy(wqb, wq_out.at[0], out_sem.at[3]))
    outs[3].start()

    for copy in [seg_copy] + kv + pp:
        copy.wait_send()
    for group in (z_copies, xl_copies, xf_copies, c_copies):
        for copy in group.values():
            copy.wait_send()
    for copy in outs:
        copy.wait()


def solution(mesh):
    nc, nx = mesh.shape["ctx"], mesh.shape["wide"] // 2

    def shards(query_rows, key_rows, value_rows, grad_out, segment, frames):
        tok, columns = query_rows.shape[1:]
        heads = columns // HD
        width = frames.shape[2]
        parts = 4
        part = tok // parts
        rows = width // nc
        vm = pltpu.VMEM
        dma = pltpu.SemaphoreType.DMA
        return pl.pallas_call(
            functools.partial(kernel, nc, nx, heads, tok, width, parts),
            name="attention_grads",
            out_shape=[
                jax.ShapeDtypeStruct((1, tok, columns), BF16),
                jax.ShapeDtypeStruct((1, tok, columns), BF16),
                jax.ShapeDtypeStruct((1, tok, columns), BF16),
                jax.ShapeDtypeStruct((1, rows, columns), F32),
            ],
            in_specs=[pl.BlockSpec(memory_space=pltpu.HBM)] * 6,
            out_specs=[pl.BlockSpec(memory_space=pl.ANY)] * 4,
            scratch_shapes=[
                vm((heads, tok, HD), BF16),
                vm((heads, 2 * tok, HD), BF16),
                vm((heads, 2 * tok, HD), BF16),
                vm((heads, tok, HD), BF16),
                vm((2, 1, tok), jnp.int32),
                vm((tok, 2 * tok), F32),
                vm((nx, tok, width), BF16),
                vm((parts, nx, part, width), BF16),
                vm((nx, width, tok), BF16),
                vm((parts, width, nx * part), BF16),
                vm((heads, tok, 2 * tok), F32),
                vm((heads, tok, 2 * tok), F32),
                vm((heads, tok, 2 * tok), BF16),
                vm((heads, tok, 2 * tok), BF16),
                vm((heads, nx, tok, HD), BF16),
                vm((heads, parts, nx, part, HD), BF16),
                vm((heads, width, HD), F32),
                vm((heads, nc, rows, HD), BF16),
                vm((heads, nc, rows, HD), BF16),
                vm((tok, columns), BF16),
                vm((tok, columns), BF16),
                vm((tok, columns), BF16),
                vm((tok, columns), F32),
                vm((tok, columns), F32),
                vm((tok, columns), F32),
                vm((tok, columns), F32),
                vm((rows, columns), F32),
                dma((4 * heads + 1,)),
                dma,
                dma((parts * nx,)),
                dma((4,)),
                dma((2 * heads + 1,)),
                dma((2 * heads + 1,)),
                dma((2,)),
                dma((2,)),
                dma((heads * parts,)),
                dma((heads * parts,)),
                dma((heads * nx,)),
                dma((heads * nx,)),
                dma((heads * parts * nx,)),
                dma((heads * parts * nx,)),
                dma((heads * nc,)),
                dma((heads * nc,)),
            ],
            compiler_params=pltpu.CompilerParams(
                collective_id=0, has_side_effects=True, vmem_limit_bytes=40 * 1024 * 1024
            ),
        )(query_rows, key_rows, value_rows, grad_out, segment, frames)

    return jax.shard_map(
        shards,
        mesh=mesh,
        in_specs=(
            P("wide", "ctx", "head"),
            P("wide", "ctx", "head"),
            P("wide", "ctx", "head"),
            P("wide", "ctx", "head"),
            P("wide", "ctx"),
            P(None, "ctx", "wide"),
        ),
        out_specs=(
            P("wide", "ctx", "head"),
            P("wide", "ctx", "head"),
            P("wide", "ctx", "head"),
            P("wide", "ctx", "head"),
        ),
        check_vma=False,
    )
```

```python
import functools

import jax
import jax.numpy as jnp
from jax import lax
from jax.experimental import pallas as pl
from jax.experimental.pallas import tpu as pltpu
from jax.sharding import PartitionSpec as P

HD = 128
MESH = pl.DeviceIdType.MESH
F32 = jnp.float32
BF16 = jnp.bfloat16
LOW = -1e30


def dot(a, b, dims):
    return lax.dot_general(a, b, (dims, ((), ())), preferred_element_type=F32)


def remote(src, dst, send, recv, where):
    return pltpu.make_async_remote_copy(
        src_ref=src, dst_ref=dst, send_sem=send, recv_sem=recv, device_id=where, device_id_type=MESH
    )


def kernel(
    nc, nh, nx, heads, tok, width,
    q_in, k_in, v_in, g_in, seg_in, fr_in,
    gq_out, gk_out, gv_out, wq_out,
    q, k, v, g, seg, bias, fl, ff, flt, fft, sc, dp, dsb, pb,
    lbuf, rbuf, fbuf, acc, rs_s, rs_r, pks, pvs, pkr, pvr,
    in_sem, fl_sem, ff_sem, kv_s, kv_r, pp_s, pp_r, z_s, z_r, y_s, y_r, xl_s, xl_r, xf_s, xf_r, c_s, c_r,
):
    c = lax.axis_index("ctx")
    w = lax.axis_index("wide")
    x = lax.rem(w, nx)
    half = w // nx
    part = tok // 2
    rows = width // nc
    nz = 2 * nh
    z = half * nh + lax.axis_index("head")
    factor = HD ** (-0.5)

    def ctx(step):
        return {"ctx": lax.rem(c + step, nc)}

    def across(step):
        return {"wide": half * nx + lax.rem(x + step, nx)}

    def along(way):
        to = lax.rem(z + (1, -1)[way] * (nh // 2) + nz, nz)
        return {"head": lax.rem(to, nh), "wide": to // nh * nx + x}

    barrier = pltpu.get_barrier_semaphore()
    others = [along(0), along(1)] + [across(j) for j in range(1, nx)] + [ctx(j) for j in range(1, nc)]
    for other in others:
        pl.semaphore_signal(barrier, inc=1, device_id=other, device_id_type=MESH)

    loads = []
    for h in range(heads):
        cols = pl.ds(h * HD, HD)
        loads.append(pltpu.make_async_copy(q_in.at[0, :, cols], q.at[h], in_sem.at[4 * h]))
        loads.append(pltpu.make_async_copy(k_in.at[0, :, cols], k.at[h, pl.ds(tok, tok)], in_sem.at[4 * h + 1]))
        loads.append(pltpu.make_async_copy(g_in.at[0, :, cols], g.at[h], in_sem.at[4 * h + 2]))
        loads.append(pltpu.make_async_copy(v_in.at[0, :, cols], v.at[h, pl.ds(tok, tok)], in_sem.at[4 * h + 3]))
    loads.append(pltpu.make_async_copy(seg_in, seg.at[1], in_sem.at[4 * heads]))
    own_frames = pltpu.make_async_copy(fr_in.at[pl.ds(half * nx, nx)], fl, fl_sem)
    far_frames = [
        pltpu.make_async_copy(
            fr_in.at[(1 - half) * nx + r, pl.ds(i * part, part)], ff.at[i, r], ff_sem.at[i * nx + r]
        )
        for i in range(2)
        for r in range(nx)
    ]
    for copy in loads + [own_frames] + far_frames:
        copy.start()
    for copy in loads:
        copy.wait()

    for h in range(heads):
        sc[h, :, tok:] = dot(q[h], k[h, tok:], ((1,), (1,))) * factor
        dp[h, :, tok:] = dot(g[h], v[h, tok:], ((1,), (1,)))

    own_frames.wait()
    for r in range(nx):
        flt[r] = fl[r].T
    for copy in far_frames:
        copy.wait()
    for i in range(2):
        fft[i] = ff[i].reshape(nx * part, width).T

    pl.semaphore_wait(barrier, len(others))

    seg_copy = remote(seg.at[1], seg.at[0], kv_s.at[2 * heads], kv_r.at[2 * heads], ctx(1))
    seg_copy.start()
    kv = []
    for h in range(heads):
        for n, ref in enumerate((k, v)):
            copy = remote(
                ref.at[h, pl.ds(tok, tok)], ref.at[h, pl.ds(0, tok)], kv_s.at[2 * h + n], kv_r.at[2 * h + n], ctx(1)
            )
            copy.start()
            kv.append(copy)

    mine = jnp.broadcast_to(seg[1], (HD, tok)).T[:, :1]
    query_place = lax.broadcasted_iota(jnp.int32, (tok, tok), 0)
    key_place = lax.broadcasted_iota(jnp.int32, (tok, tok), 1)
    bias[:, tok:] = jnp.where((mine == seg[1]) & (key_place <= query_place), 0.0, LOW)
    seg_copy.wait_recv()
    bias[:, :tok] = jnp.where((mine == seg[0]) & (c > 0), 0.0, LOW)

    y_copies = {}
    z_copies = {}
    xl_copies = {}
    for h in range(heads):
        kv[2 * h].wait_recv()
        sc[h, :, :tok] = dot(q[h], k[h, :tok], ((1,), (1,))) * factor
        kv[2 * h + 1].wait_recv()
        dp[h, :, :tok] = dot(g[h], v[h, :tok], ((1,), (1,)))
        scores = sc[h] + bias[...]
        row_max = jnp.max(scores, axis=1, keepdims=True)
        weight = jnp.exp(scores - row_max)
        prob = weight * (1.0 / jnp.sum(weight, axis=1, keepdims=True))
        grad_prob = dp[h]
        row_delta = jnp.sum(prob * grad_prob, axis=1, keepdims=True)
        grad_score = (prob * (grad_prob - row_delta)).astype(BF16)
        dsb[h] = grad_score
        pb[h] = prob.astype(BF16)
        grad_query = (dot(grad_score, k[h], ((1,), (0,))) * factor).astype(BF16)
        lbuf[h, x] = grad_query
        gq_out[0, :, h * HD : (h + 1) * HD] = grad_query
        for i in range(2):
            copy = remote(
                lbuf.at[h, x, pl.ds(i * part, part)], rbuf.at[h, i], y_s.at[2 * h + i], y_r.at[2 * h + i], along(i)
            )
            copy.start()
            y_copies[h, i] = copy
        for j in range(1, nx):
            copy = remote(lbuf.at[h, x], lbuf.at[h, x], xl_s.at[h * nx + j], xl_r.at[h * nx + j], across(j))
            copy.start()
            xl_copies[h, j] = copy

    for h in range(heads):
        cols = slice(h * HD, (h + 1) * HD)
        pks[:, cols] = dot(dsb[h, :, :tok], q[h], ((0,), (0,)))
        pvs[:, cols] = dot(pb[h, :, :tok], g[h], ((0,), (0,)))
    pp = [
        remote(pks, pkr, pp_s.at[0], pp_r.at[0], ctx(nc - 1)),
        remote(pvs, pvr, pp_s.at[1], pp_r.at[1], ctx(nc - 1)),
    ]
    for copy in pp:
        copy.start()

    def relay(h):
        for i in range(2):
            y_copies[h, i].wait_recv()
            copy = remote(rbuf.at[h, i], fbuf.at[h, i, x], z_s.at[2 * h + i], z_r.at[2 * h + i], along(i))
            copy.start()
            z_copies[h, i] = copy

    def near(h):
        for j in range(1, nx):
            xl_copies[h, j].wait_recv()
        total = dot(flt[0], lbuf[h, 0], ((1,), (0,)))
        for r in range(1, nx):
            total += dot(flt[r], lbuf[h, r], ((1,), (0,)))
        acc[h] = total

    for h in range(heads):
        relay(h)
    for h in range(heads):
        near(h)

    for copy in pp:
        copy.wait_recv()
    for h in range(heads):
        cols = slice(h * HD, (h + 1) * HD)
        own_key = dot(dsb[h, :, tok:], q[h], ((0,), (0,)))
        own_value = dot(pb[h, :, tok:], g[h], ((0,), (0,)))
        gk_out[0, :, cols] = ((own_key + pkr[:, cols]) * factor).astype(BF16)
        gv_out[0, :, cols] = (own_value + pvr[:, cols]).astype(BF16)

    xf_copies = {}
    c_copies = {}
    order = [(h, i) for h in range(heads) for i in range(2)]

    def pass_on(h, i):
        z_copies[h, i].wait_recv()
        for j in range(1, nx):
            n = (2 * h + i) * nx + j
            copy = remote(fbuf.at[h, i, x], fbuf.at[h, i, x], xf_s.at[n], xf_r.at[n], across(j))
            copy.start()
            xf_copies[h, i, j] = copy

    def add(h, i):
        for j in range(1, nx):
            xf_copies[h, i, j].wait_recv()
        total = acc[h] + dot(fft[i], fbuf[h, i].reshape(nx * part, HD), ((1,), (0,)))
        acc[h] = total
        if i == 1:
            rs_s[h] = total.astype(BF16).reshape(nc, rows, HD)
            for j in range(1, nc):
                to = lax.rem(c + j, nc)
                copy = remote(rs_s.at[h, to], rs_r.at[h, j], c_s.at[h * nc + j], c_r.at[h * nc + j], ctx(j))
                copy.start()
                c_copies[h, j] = copy

    pass_on(*order[0])
    for n in range(1, len(order)):
        pass_on(*order[n])
        add(*order[n - 1])
    add(*order[-1])

    for h in range(heads):
        total = acc[h, pl.ds(pl.multiple_of(c * rows, rows), rows)]
        for j in range(1, nc):
            c_copies[h, j].wait_recv()
            total += rs_r[h, j].astype(F32)
        wq_out[0, :, h * HD : (h + 1) * HD] = total

    for copy in [seg_copy] + kv + pp:
        copy.wait_send()
    for group in (y_copies, z_copies, xl_copies, xf_copies, c_copies):
        for copy in group.values():
            copy.wait_send()


def store(*refs):
    n = len(refs) // 2
    for i in range(n):
        pltpu.make_async_copy(refs[i], refs[n + i], refs[-1].at[i]).start()
    for i in range(n):
        pltpu.make_async_copy(refs[i], refs[n + i], refs[-1].at[i]).wait()


def solution(mesh):
    nc, nh, nx = mesh.shape["ctx"], mesh.shape["head"], mesh.shape["wide"] // 2

    def shards(query_rows, key_rows, value_rows, grad_out, segment, frames):
        tok, columns = query_rows.shape[1:]
        heads = columns // HD
        width = frames.shape[2]
        part = tok // 2
        rows = width // nc
        vm = pltpu.VMEM
        dma = pltpu.SemaphoreType.DMA
        shapes = [(1, tok, columns)] * 3 + [(1, rows, columns)]
        types = [BF16] * 3 + [F32]
        results = pl.pallas_call(
            functools.partial(kernel, nc, nh, nx, heads, tok, width),
            name="attention_grads",
            out_shape=[vm(shape, kind) for shape, kind in zip(shapes, types)],
            in_specs=[pl.BlockSpec(memory_space=pl.ANY)] * 6,
            out_specs=[pl.BlockSpec(memory_space=vm)] * 4,
            scratch_shapes=[
                vm((heads, tok, HD), BF16),
                vm((heads, 2 * tok, HD), BF16),
                vm((heads, 2 * tok, HD), BF16),
                vm((heads, tok, HD), BF16),
                vm((2, 1, tok), jnp.int32),
                vm((tok, 2 * tok), F32),
                vm((nx, tok, width), BF16),
                vm((2, nx, part, width), BF16),
                vm((nx, width, tok), BF16),
                vm((2, width, nx * part), BF16),
                vm((heads, tok, 2 * tok), F32),
                vm((heads, tok, 2 * tok), F32),
                vm((heads, tok, 2 * tok), BF16),
                vm((heads, tok, 2 * tok), BF16),
                vm((heads, nx, tok, HD), BF16),
                vm((heads, 2, part, HD), BF16),
                vm((heads, 2, nx, part, HD), BF16),
                vm((heads, width, HD), F32),
                vm((heads, nc, rows, HD), BF16),
                vm((heads, nc, rows, HD), BF16),
                vm((tok, columns), F32),
                vm((tok, columns), F32),
                vm((tok, columns), F32),
                vm((tok, columns), F32),
                dma((4 * heads + 1,)),
                dma,
                dma((2 * nx,)),
                dma((2 * heads + 1,)),
                dma((2 * heads + 1,)),
                dma((2,)),
                dma((2,)),
                dma((2 * heads,)),
                dma((2 * heads,)),
                dma((2 * heads,)),
                dma((2 * heads,)),
                dma((heads * nx,)),
                dma((heads * nx,)),
                dma((2 * heads * nx,)),
                dma((2 * heads * nx,)),
                dma((heads * nc,)),
                dma((heads * nc,)),
            ],
            compiler_params=pltpu.CompilerParams(
                collective_id=0, has_side_effects=True, vmem_limit_bytes=60 * 1024 * 1024
            ),
        )(query_rows, key_rows, value_rows, grad_out, segment, frames)
        return pl.pallas_call(
            store,
            name="store",
            out_shape=[jax.ShapeDtypeStruct(shape, kind) for shape, kind in zip(shapes, types)],
            in_specs=[pl.BlockSpec(memory_space=pl.ANY)] * 4,
            out_specs=[pl.BlockSpec(memory_space=pl.ANY)] * 4,
            scratch_shapes=[dma((4,))],
            compiler_params=pltpu.CompilerParams(vmem_limit_bytes=1024 * 1024),
        )(*results)

    return jax.shard_map(
        shards,
        mesh=mesh,
        in_specs=(
            P("wide", "ctx", "head"),
            P("wide", "ctx", "head"),
            P("wide", "ctx", "head"),
            P("wide", "ctx", "head"),
            P("wide", "ctx"),
            P(None, "ctx", "wide"),
        ),
        out_specs=(
            P("wide", "ctx", "head"),
            P("wide", "ctx", "head"),
            P("wide", "ctx", "head"),
            P("wide", "ctx", "head"),
        ),
        check_vma=False,
    )
```

```python
import functools

import jax
import jax.numpy as jnp
from jax import lax
from jax.experimental import pallas as pl
from jax.experimental.pallas import tpu as pltpu
from jax.sharding import PartitionSpec as P

HD = 128
MESH = pl.DeviceIdType.MESH
F32 = jnp.float32
BF16 = jnp.bfloat16
LOW = -1e30


def dot(a, b, dims):
    return lax.dot_general(a, b, (dims, ((), ())), preferred_element_type=F32)


def remote(src, dst, send, recv, where):
    return pltpu.make_async_remote_copy(
        src_ref=src, dst_ref=dst, send_sem=send, recv_sem=recv, device_id=where, device_id_type=MESH
    )


def kernel(
    nc, nh, nx, hops, heads, tok, width,
    q_in, k_in, v_in, g_in, seg_in, fr_in,
    gq_out, gk_out, gv_out, wq_out,
    q, kv, g, seg, bias, fl, ff, flt, fft, sc, dp, dsb, pb,
    lbuf, rbuf, fbuf, acc, rs_s, rs_r, pks, pvs, pkr, pvr,
    in_sem, fl_sem, ff_sem, kv_s, kv_r, pp_s, pp_r, z_s, z_r, xl_s, xl_r, xf_s, xf_r, c_s, c_r,
):
    c = lax.axis_index("ctx")
    w = lax.axis_index("wide")
    x = lax.rem(w, nx)
    half = w // nx
    rows = width // nc
    nz = 2 * nh
    z = half * nh + lax.axis_index("head")
    part = tok // 2
    factor = HD ** (-0.5)

    def ctx(step):
        return {"ctx": lax.rem(c + step, nc)}

    def across(step):
        return {"wide": half * nx + lax.rem(x + step, nx)}

    def along(way):
        to = lax.rem(z + (1, -1)[way] * (nh // hops) + nz, nz)
        return {"head": lax.rem(to, nh), "wide": to // nh * nx + x}

    barrier = pltpu.get_barrier_semaphore()
    others = [along(0), along(1)] + [across(j) for j in range(1, nx)] + [ctx(j) for j in range(1, nc)]
    for other in others:
        pl.semaphore_signal(barrier, inc=1, device_id=other, device_id_type=MESH)

    loads = []
    for h in range(heads):
        cols = pl.ds(h * HD, HD)
        loads.append(pltpu.make_async_copy(q_in.at[0, :, cols], q.at[h], in_sem.at[4 * h]))
        loads.append(pltpu.make_async_copy(k_in.at[0, :, cols], kv.at[h, 0, pl.ds(tok, tok)], in_sem.at[4 * h + 1]))
        loads.append(pltpu.make_async_copy(g_in.at[0, :, cols], g.at[h], in_sem.at[4 * h + 2]))
        loads.append(pltpu.make_async_copy(v_in.at[0, :, cols], kv.at[h, 1, pl.ds(tok, tok)], in_sem.at[4 * h + 3]))
    loads.append(pltpu.make_async_copy(seg_in, seg.at[1], in_sem.at[4 * heads]))
    own_frames = pltpu.make_async_copy(fr_in.at[pl.ds(half * nx, nx)], fl, fl_sem)
    far_frames = pltpu.make_async_copy(fr_in.at[pl.ds((1 - half) * nx, nx)], ff, ff_sem)
    for copy in loads + [own_frames, far_frames]:
        copy.start()
    for copy in loads:
        copy.wait()

    @pl.when(c == 0)
    def _():
        seg[0] = jnp.zeros_like(seg[0])
        for h in range(heads):
            for n in range(2):
                kv[h, n, :tok] = jnp.zeros((tok, HD), BF16)

    @pl.when(c == nc - 1)
    def _():
        pkr[...] = jnp.zeros_like(pkr)
        pvr[...] = jnp.zeros_like(pvr)

    for h in range(heads):
        sc[h, :, tok:] = dot(q[h], kv[h, 0, tok:], ((1,), (1,))) * factor
        dp[h, :, tok:] = dot(g[h], kv[h, 1, tok:], ((1,), (1,)))


    pl.semaphore_wait(barrier, len(others))

    kv_copies = [
        remote(kv.at[h, :, pl.ds(tok, tok)], kv.at[h, :, pl.ds(0, tok)], kv_s.at[h], kv_r.at[h], ctx(1))
        for h in range(heads)
    ]
    seg_copy = remote(seg.at[1], seg.at[0], kv_s.at[heads], kv_r.at[heads], ctx(1))
    first = [seg_copy] + kv_copies
    has_prior, has_later = c > 0, c < nc - 1

    @pl.when(has_later)
    def _():
        for copy in first:
            copy.start()


    mine = jnp.broadcast_to(seg[1], (HD, tok)).T[:, :1]
    query_place = lax.broadcasted_iota(jnp.int32, (tok, tok), 0)
    key_place = lax.broadcasted_iota(jnp.int32, (tok, tok), 1)
    bias[:, tok:] = jnp.where((mine == seg[1]) & (key_place <= query_place), 0.0, LOW)
    pl.when(has_prior)(seg_copy.wait_recv)
    bias[:, :tok] = jnp.where((mine == seg[0]) & (c > 0), 0.0, LOW)

    z_copies = {}
    xl_copies = {}

    def hop(h, way, n, src):
        dst = fbuf.at[h, x, pl.ds(way * part, part)] if n == hops - 1 else rbuf.at[h, way, n]
        m = (2 * h + way) * hops + n
        copy = remote(src, dst, z_s.at[m], z_r.at[m], along(way))
        copy.start()
        z_copies[h, way, n] = copy

    for h in range(heads):
        pl.when(has_prior)(kv_copies[h].wait_recv)
        sc[h, :, :tok] = dot(q[h], kv[h, 0, :tok], ((1,), (1,))) * factor
        dp[h, :, :tok] = dot(g[h], kv[h, 1, :tok], ((1,), (1,)))
        scores = sc[h] + bias[...]
        row_max = jnp.max(scores, axis=1, keepdims=True)
        weight = jnp.exp(scores - row_max)
        prob = weight * (1.0 / jnp.sum(weight, axis=1, keepdims=True))
        grad_prob = dp[h]
        row_delta = jnp.sum(prob * grad_prob, axis=1, keepdims=True)
        grad_score = (prob * (grad_prob - row_delta)).astype(BF16)
        dsb[h] = grad_score
        pb[h] = prob.astype(BF16)
        grad_query = (dot(grad_score, kv[h, 0], ((1,), (0,))) * factor).astype(BF16)
        lbuf[h, x] = grad_query
        gq_out[0, :, h * HD : (h + 1) * HD] = grad_query
        for way in range(2):
            hop(h, way, 0, lbuf.at[h, x, pl.ds(way * part, part)])

    for h in range(heads):
        for j in range(1, nx):
            copy = remote(lbuf.at[h, x], lbuf.at[h, x], xl_s.at[h * nx + j], xl_r.at[h * nx + j], across(j))
            copy.start()
            xl_copies[h, j] = copy

    for h in range(heads):
        cols = slice(h * HD, (h + 1) * HD)
        pks[:, cols] = dot(dsb[h, :, :tok], q[h], ((0,), (0,)))
        pvs[:, cols] = dot(pb[h, :, :tok], g[h], ((0,), (0,)))
    pp = [
        remote(pks, pkr, pp_s.at[0], pp_r.at[0], ctx(nc - 1)),
        remote(pvs, pvr, pp_s.at[1], pp_r.at[1], ctx(nc - 1)),
    ]

    @pl.when(has_prior)
    def _():
        for copy in pp:
            copy.start()


    def near(h):
        for j in range(1, nx):
            xl_copies[h, j].wait_recv()
        total = dot(flt[0], lbuf[h, 0], ((1,), (0,)))
        for r in range(1, nx):
            total += dot(flt[r], lbuf[h, r], ((1,), (0,)))
        acc[h] = total

    own_frames.wait()
    for r in range(nx):
        flt[r] = fl[r].T
    far_frames.wait()
    for r in range(nx):
        fft[r] = ff[r].T

    for n in range(1, hops):
        for h in range(heads):
            for way in range(2):
                z_copies[h, way, n - 1].wait_recv()
                hop(h, way, n, rbuf.at[h, way, n - 1])
    for h in range(heads):
        near(h)

    @pl.when(has_later)
    def _():
        for copy in pp:
            copy.wait_recv()

    for h in range(heads):
        cols = slice(h * HD, (h + 1) * HD)
        own_key = dot(dsb[h, :, tok:], q[h], ((0,), (0,)))
        own_value = dot(pb[h, :, tok:], g[h], ((0,), (0,)))
        gk_out[0, :, cols] = ((own_key + pkr[:, cols]) * factor).astype(BF16)
        gv_out[0, :, cols] = (own_value + pvr[:, cols]).astype(BF16)

    xf_copies = {}
    c_copies = {}

    def pass_on(h):
        for way in range(2):
            z_copies[h, way, hops - 1].wait_recv()
        for j in range(1, nx):
            copy = remote(fbuf.at[h, x], fbuf.at[h, x], xf_s.at[h * nx + j], xf_r.at[h * nx + j], across(j))
            copy.start()
            xf_copies[h, j] = copy

    def add(h):
        for j in range(1, nx):
            xf_copies[h, j].wait_recv()
        total = acc[h]
        for r in range(nx):
            total += dot(fft[r], fbuf[h, r], ((1,), (0,)))
        acc[h] = total
        rs_s[:, :, h * HD : (h + 1) * HD] = total.astype(BF16).reshape(nc, rows, HD)

    for h in range(heads):
        pass_on(h)
    for h in range(heads):
        add(h)
    for j in range(1, nc):
        copy = remote(rs_s.at[lax.rem(c + j, nc)], rs_r.at[j], c_s.at[j], c_r.at[j], ctx(j))
        copy.start()
        c_copies[j] = copy
    own_rows = pl.ds(pl.multiple_of(c * rows, rows), rows)
    total = jnp.concatenate([acc[h, own_rows] for h in range(heads)], axis=1)
    for j in range(1, nc):
        c_copies[j].wait_recv()
        total += rs_r[j].astype(F32)
    wq_out[0] = total

    @pl.when(has_later)
    def _():
        for copy in first:
            copy.wait_send()

    @pl.when(has_prior)
    def _():
        for copy in pp:
            copy.wait_send()

    for group in (z_copies, xl_copies, xf_copies, c_copies):
        for copy in group.values():
            copy.wait_send()


def store(*refs):
    n = len(refs) // 2
    for i in range(n):
        pltpu.make_async_copy(refs[i], refs[n + i], refs[-1].at[i]).start()
    for i in range(n):
        pltpu.make_async_copy(refs[i], refs[n + i], refs[-1].at[i]).wait()


def solution(mesh):
    nc, nh, nx = mesh.shape["ctx"], mesh.shape["head"], mesh.shape["wide"] // 2

    def shards(query_rows, key_rows, value_rows, grad_out, segment, frames):
        tok, columns = query_rows.shape[1:]
        heads = columns // HD
        width = frames.shape[2]
        rows = width // nc
        vm = pltpu.VMEM
        dma = pltpu.SemaphoreType.DMA
        shapes = [(1, tok, columns)] * 3 + [(1, rows, columns)]
        types = [BF16] * 3 + [F32]
        results = pl.pallas_call(
            functools.partial(kernel, nc, nh, nx, 4, heads, tok, width),
            name="attention_grads",
            out_shape=[vm(shape, kind) for shape, kind in zip(shapes, types)],
            in_specs=[pl.BlockSpec(memory_space=pl.ANY)] * 6,
            out_specs=[pl.BlockSpec(memory_space=vm)] * 4,
            scratch_shapes=[
                vm((heads, tok, HD), BF16),
                vm((heads, 2, 2 * tok, HD), BF16),
                vm((heads, tok, HD), BF16),
                vm((2, 1, tok), jnp.int32),
                vm((tok, 2 * tok), F32),
                vm((nx, tok, width), BF16),
                vm((nx, tok, width), BF16),
                vm((nx, width, tok), BF16),
                vm((nx, width, tok), BF16),
                vm((heads, tok, 2 * tok), F32),
                vm((heads, tok, 2 * tok), F32),
                vm((heads, tok, 2 * tok), BF16),
                vm((heads, tok, 2 * tok), BF16),
                vm((heads, nx, tok, HD), BF16),
                vm((heads, 2, 3, tok // 2, HD), BF16),
                vm((heads, nx, tok, HD), BF16),
                vm((heads, width, HD), F32),
                vm((nc, rows, columns), BF16),
                vm((nc, rows, columns), BF16),
                vm((tok, columns), F32),
                vm((tok, columns), F32),
                vm((tok, columns), F32),
                vm((tok, columns), F32),
                dma((4 * heads + 1,)),
                dma,
                dma,
                dma((heads + 1,)),
                dma((heads + 1,)),
                dma((2,)),
                dma((2,)),
                dma((heads * 8,)),
                dma((heads * 8,)),
                dma((heads * nx,)),
                dma((heads * nx,)),
                dma((heads * nx,)),
                dma((heads * nx,)),
                dma((nc,)),
                dma((nc,)),
            ],
            compiler_params=pltpu.CompilerParams(
                collective_id=0, has_side_effects=True, vmem_limit_bytes=60 * 1024 * 1024
            ),
        )(query_rows, key_rows, value_rows, grad_out, segment, frames)
        return pl.pallas_call(
            store,
            name="store",
            out_shape=[jax.ShapeDtypeStruct(shape, kind) for shape, kind in zip(shapes, types)],
            in_specs=[pl.BlockSpec(memory_space=pl.ANY)] * 4,
            out_specs=[pl.BlockSpec(memory_space=pl.ANY)] * 4,
            scratch_shapes=[dma((4,))],
            compiler_params=pltpu.CompilerParams(vmem_limit_bytes=1024 * 1024),
        )(*results)

    return jax.shard_map(
        shards,
        mesh=mesh,
        in_specs=(
            P("wide", "ctx", "head"),
            P("wide", "ctx", "head"),
            P("wide", "ctx", "head"),
            P("wide", "ctx", "head"),
            P("wide", "ctx"),
            P(None, "ctx", "wide"),
        ),
        out_specs=(
            P("wide", "ctx", "head"),
            P("wide", "ctx", "head"),
            P("wide", "ctx", "head"),
            P("wide", "ctx", "head"),
        ),
        check_vma=False,
    )
```

```python
import functools

import jax
import jax.numpy as jnp
from jax import lax
from jax.experimental import pallas as pl
from jax.experimental.pallas import tpu as pltpu
from jax.sharding import PartitionSpec as P

HD = 128
MESH = pl.DeviceIdType.MESH
F32 = jnp.float32
BF16 = jnp.bfloat16
LOW = -1e30


def dot(a, b, dims):
    return lax.dot_general(a, b, (dims, ((), ())), preferred_element_type=F32)


def remote(src, dst, send, recv, where):
    return pltpu.make_async_remote_copy(
        src_ref=src, dst_ref=dst, send_sem=send, recv_sem=recv, device_id=where, device_id_type=MESH
    )


def kernel(
    nc, nh, nx, hops, heads, tok, width,
    q_in, k_in, v_in, g_in, seg_in, fr_in,
    gq_out, gk_out, gv_out, wq_out,
    q, kv, g, seg, bias, fl, ff, flt, fft, sc, dp, dsb, pb,
    lbuf, rbuf, fbuf, acc, rs_s, rs_r, pks, pvs, pkr, pvr,
    in_sem, fl_sem, ff_sem, kv_s, kv_r, pp_s, pp_r, z_s, z_r, xl_s, xl_r, xf_s, xf_r, c_s, c_r,
):
    c = lax.axis_index("ctx")
    w = lax.axis_index("wide")
    x = lax.rem(w, nx)
    half = w // nx
    rows = width // nc
    nz = 2 * nh
    z = half * nh + lax.axis_index("head")
    part = tok // 2
    factor = HD ** (-0.5)

    def ctx(step):
        return {"ctx": lax.rem(c + step, nc)}

    def across(step):
        return {"wide": half * nx + lax.rem(x + step, nx)}

    def along(way):
        to = lax.rem(z + (1, -1)[way] * (nh // hops) + nz, nz)
        return {"head": lax.rem(to, nh), "wide": to // nh * nx + x}

    barrier = pltpu.get_barrier_semaphore()
    others = [along(0), along(1)] + [across(j) for j in range(1, nx)] + [ctx(j) for j in range(1, nc)]
    for other in others:
        pl.semaphore_signal(barrier, inc=1, device_id=other, device_id_type=MESH)

    loads = []
    for h in range(heads):
        cols = pl.ds(h * HD, HD)
        loads.append(pltpu.make_async_copy(q_in.at[0, :, cols], q.at[h], in_sem.at[4 * h]))
        loads.append(pltpu.make_async_copy(k_in.at[0, :, cols], kv.at[h, 0, pl.ds(tok, tok)], in_sem.at[4 * h + 1]))
        loads.append(pltpu.make_async_copy(g_in.at[0, :, cols], g.at[h], in_sem.at[4 * h + 2]))
        loads.append(pltpu.make_async_copy(v_in.at[0, :, cols], kv.at[h, 1, pl.ds(tok, tok)], in_sem.at[4 * h + 3]))
    loads.append(pltpu.make_async_copy(seg_in, seg.at[1], in_sem.at[4 * heads]))
    own_frames = pltpu.make_async_copy(fr_in.at[pl.ds(half * nx, nx)], fl, fl_sem)
    far_frames = pltpu.make_async_copy(fr_in.at[pl.ds((1 - half) * nx, nx)], ff, ff_sem)
    for copy in loads + [own_frames, far_frames]:
        copy.start()
    for copy in loads:
        copy.wait()

    @pl.when(c == 0)
    def _():
        seg[0] = jnp.zeros_like(seg[0])
        for h in range(heads):
            for n in range(2):
                kv[h, n, :tok] = jnp.zeros((tok, HD), BF16)

    @pl.when(c == nc - 1)
    def _():
        pkr[...] = jnp.zeros_like(pkr)
        pvr[...] = jnp.zeros_like(pvr)

    for h in range(heads):
        sc[h, :, tok:] = dot(q[h], kv[h, 0, tok:], ((1,), (1,))) * factor
        dp[h, :, tok:] = dot(g[h], kv[h, 1, tok:], ((1,), (1,)))


    pl.semaphore_wait(barrier, len(others))

    kv_copies = [
        remote(kv.at[h, :, pl.ds(tok, tok)], kv.at[h, :, pl.ds(0, tok)], kv_s.at[h], kv_r.at[h], ctx(1))
        for h in range(heads)
    ]
    seg_copy = remote(seg.at[1], seg.at[0], kv_s.at[heads], kv_r.at[heads], ctx(1))
    first = [seg_copy] + kv_copies
    has_prior, has_later = c > 0, c < nc - 1

    @pl.when(has_later)
    def _():
        for copy in first:
            copy.start()


    mine = jnp.broadcast_to(seg[1], (HD, tok)).T[:, :1]
    query_place = lax.broadcasted_iota(jnp.int32, (tok, tok), 0)
    key_place = lax.broadcasted_iota(jnp.int32, (tok, tok), 1)
    bias[:, tok:] = jnp.where((mine == seg[1]) & (key_place <= query_place), 0.0, LOW)
    pl.when(has_prior)(seg_copy.wait_recv)
    bias[:, :tok] = jnp.where((mine == seg[0]) & (c > 0), 0.0, LOW)

    z_copies = {}
    xl_copies = {}

    def hop(h, way, n, src):
        dst = fbuf.at[h, x, pl.ds(way * part, part)] if n == hops - 1 else rbuf.at[h, way, n]
        m = (2 * h + way) * hops + n
        copy = remote(src, dst, z_s.at[m], z_r.at[m], along(way))
        copy.start()
        z_copies[h, way, n] = copy

    for h in range(heads):
        pl.when(has_prior)(kv_copies[h].wait_recv)
        sc[h, :, :tok] = dot(q[h], kv[h, 0, :tok], ((1,), (1,))) * factor
        dp[h, :, :tok] = dot(g[h], kv[h, 1, :tok], ((1,), (1,)))
        scores = sc[h] + bias[...]
        row_max = jnp.max(scores, axis=1, keepdims=True)
        weight = jnp.exp(scores - row_max)
        prob = weight * (1.0 / jnp.sum(weight, axis=1, keepdims=True))
        grad_prob = dp[h]
        row_delta = jnp.sum(prob * grad_prob, axis=1, keepdims=True)
        grad_score = (prob * (grad_prob - row_delta)).astype(BF16)
        dsb[h] = grad_score
        pb[h] = prob.astype(BF16)
        grad_query = (dot(grad_score, kv[h, 0], ((1,), (0,))) * factor).astype(BF16)
        lbuf[h, x] = grad_query
        gq_out[0, :, h * HD : (h + 1) * HD] = grad_query
        for way in range(2):
            hop(h, way, 0, lbuf.at[h, x, pl.ds(way * part, part)])

    for j in range(1, nx):
        copy = remote(lbuf.at[:, x], lbuf.at[:, x], xl_s.at[j], xl_r.at[j], across(j))
        copy.start()
        xl_copies[j] = copy

    for h in range(heads):
        cols = slice(h * HD, (h + 1) * HD)
        pks[:, cols] = dot(dsb[h, :, :tok], q[h], ((0,), (0,)))
        pvs[:, cols] = dot(pb[h, :, :tok], g[h], ((0,), (0,)))
    pp = [
        remote(pks, pkr, pp_s.at[0], pp_r.at[0], ctx(nc - 1)),
        remote(pvs, pvr, pp_s.at[1], pp_r.at[1], ctx(nc - 1)),
    ]

    @pl.when(has_prior)
    def _():
        for copy in pp:
            copy.start()


    def near(h):
        total = dot(flt[0], lbuf[h, 0], ((1,), (0,)))
        for r in range(1, nx):
            total += dot(flt[r], lbuf[h, r], ((1,), (0,)))
        acc[h] = total

    def relay(n):
        for h in range(heads):
            for way in range(2):
                z_copies[h, way, n - 1].wait_recv()
                hop(h, way, n, rbuf.at[h, way, n - 1])

    relay(1)
    own_frames.wait()
    for r in range(nx):
        flt[r] = fl[r].T
    if hops > 2:
        relay(2)
    far_frames.wait()
    for r in range(nx):
        fft[r] = ff[r].T

    for n in range(3, hops):
        relay(n)

    for j in range(1, nx):
        xl_copies[j].wait_recv()
    for h in range(heads):
        near(h)

    @pl.when(has_later)
    def _():
        for copy in pp:
            copy.wait_recv()

    for h in range(heads):
        cols = slice(h * HD, (h + 1) * HD)
        own_key = dot(dsb[h, :, tok:], q[h], ((0,), (0,)))
        own_value = dot(pb[h, :, tok:], g[h], ((0,), (0,)))
        gk_out[0, :, cols] = ((own_key + pkr[:, cols]) * factor).astype(BF16)
        gv_out[0, :, cols] = (own_value + pvr[:, cols]).astype(BF16)

    xf_copies = {}
    c_copies = {}

    def pass_on(h):
        for way in range(2):
            z_copies[h, way, hops - 1].wait_recv()
        for j in range(1, nx):
            copy = remote(fbuf.at[h, x], fbuf.at[h, x], xf_s.at[h * nx + j], xf_r.at[h * nx + j], across(j))
            copy.start()
            xf_copies[h, j] = copy

    def add(h):
        total = acc[h] + dot(fft[x], fbuf[h, x], ((1,), (0,)))
        for j in range(1, nx):
            xf_copies[h, j].wait_recv()
            r = lax.rem(x - j + nx, nx)
            total += dot(fft[r], fbuf[h, r], ((1,), (0,)))
        acc[h] = total
        rs_s[h] = total.astype(BF16).reshape(nc, rows, HD)
        for j in range(1, nc):
            n = h * nc + j
            copy = remote(rs_s.at[h, lax.rem(c + j, nc)], rs_r.at[h, j], c_s.at[n], c_r.at[n], ctx(j))
            copy.start()
            c_copies[h, j] = copy

    for h in range(heads):
        pass_on(h)
    for h in range(heads):
        add(h)
    own_rows = pl.ds(pl.multiple_of(c * rows, rows), rows)
    for h in range(heads):
        total = acc[h, own_rows]
        for j in range(1, nc):
            c_copies[h, j].wait_recv()
            total += rs_r[h, j].astype(F32)
        wq_out[0, :, h * HD : (h + 1) * HD] = total

    @pl.when(has_later)
    def _():
        for copy in first:
            copy.wait_send()

    @pl.when(has_prior)
    def _():
        for copy in pp:
            copy.wait_send()

    for group in (z_copies, xl_copies, xf_copies, c_copies):
        for copy in group.values():
            copy.wait_send()


def store(*refs):
    n = len(refs) // 2
    for i in range(n):
        pltpu.make_async_copy(refs[i], refs[n + i], refs[-1].at[i]).start()
    for i in range(n):
        pltpu.make_async_copy(refs[i], refs[n + i], refs[-1].at[i]).wait()


def solution(mesh):
    nc, nh, nx = mesh.shape["ctx"], mesh.shape["head"], mesh.shape["wide"] // 2

    def shards(query_rows, key_rows, value_rows, grad_out, segment, frames):
        tok, columns = query_rows.shape[1:]
        heads = columns // HD
        width = frames.shape[2]
        rows = width // nc
        vm = pltpu.VMEM
        dma = pltpu.SemaphoreType.DMA
        shapes = [(1, tok, columns)] * 3 + [(1, rows, columns)]
        types = [BF16] * 3 + [F32]
        results = pl.pallas_call(
            functools.partial(kernel, nc, nh, nx, 4, heads, tok, width),
            name="attention_grads",
            out_shape=[vm(shape, kind) for shape, kind in zip(shapes, types)],
            in_specs=[pl.BlockSpec(memory_space=pl.ANY)] * 6,
            out_specs=[pl.BlockSpec(memory_space=vm)] * 4,
            scratch_shapes=[
                vm((heads, tok, HD), BF16),
                vm((heads, 2, 2 * tok, HD), BF16),
                vm((heads, tok, HD), BF16),
                vm((2, 1, tok), jnp.int32),
                vm((tok, 2 * tok), F32),
                vm((nx, tok, width), BF16),
                vm((nx, tok, width), BF16),
                vm((nx, width, tok), BF16),
                vm((nx, width, tok), BF16),
                vm((heads, tok, 2 * tok), F32),
                vm((heads, tok, 2 * tok), F32),
                vm((heads, tok, 2 * tok), BF16),
                vm((heads, tok, 2 * tok), BF16),
                vm((heads, nx, tok, HD), BF16),
                vm((heads, 2, 3, tok // 2, HD), BF16),
                vm((heads, nx, tok, HD), BF16),
                vm((heads, width, HD), F32),
                vm((heads, nc, rows, HD), BF16),
                vm((heads, nc, rows, HD), BF16),
                vm((tok, columns), F32),
                vm((tok, columns), F32),
                vm((tok, columns), F32),
                vm((tok, columns), F32),
                dma((4 * heads + 1,)),
                dma,
                dma,
                dma((heads + 1,)),
                dma((heads + 1,)),
                dma((2,)),
                dma((2,)),
                dma((heads * 8,)),
                dma((heads * 8,)),
                dma((nx,)),
                dma((nx,)),
                dma((heads * nx,)),
                dma((heads * nx,)),
                dma((heads * nc,)),
                dma((heads * nc,)),
            ],
            compiler_params=pltpu.CompilerParams(
                collective_id=0, has_side_effects=True, vmem_limit_bytes=60 * 1024 * 1024
            ),
        )(query_rows, key_rows, value_rows, grad_out, segment, frames)
        return pl.pallas_call(
            store,
            name="store",
            out_shape=[jax.ShapeDtypeStruct(shape, kind) for shape, kind in zip(shapes, types)],
            in_specs=[pl.BlockSpec(memory_space=pl.ANY)] * 4,
            out_specs=[pl.BlockSpec(memory_space=pl.ANY)] * 4,
            scratch_shapes=[dma((4,))],
            compiler_params=pltpu.CompilerParams(vmem_limit_bytes=1024 * 1024),
        )(*results)

    return jax.shard_map(
        shards,
        mesh=mesh,
        in_specs=(
            P("wide", "ctx", "head"),
            P("wide", "ctx", "head"),
            P("wide", "ctx", "head"),
            P("wide", "ctx", "head"),
            P("wide", "ctx"),
            P(None, "ctx", "wide"),
        ),
        out_specs=(
            P("wide", "ctx", "head"),
            P("wide", "ctx", "head"),
            P("wide", "ctx", "head"),
            P("wide", "ctx", "head"),
        ),
        check_vma=False,
    )
```

```python
import functools

import jax
import jax.numpy as jnp
from jax import lax
from jax.experimental import pallas as pl
from jax.experimental.pallas import tpu as pltpu
from jax.sharding import PartitionSpec as P

HD = 128
MESH = pl.DeviceIdType.MESH
F32 = jnp.float32
BF16 = jnp.bfloat16
LOW = -1e30


def dot(a, b, dims):
    return lax.dot_general(a, b, (dims, ((), ())), preferred_element_type=F32)


def remote(src, dst, send, recv, where):
    return pltpu.make_async_remote_copy(
        src_ref=src, dst_ref=dst, send_sem=send, recv_sem=recv, device_id=where, device_id_type=MESH
    )


def kernel(
    nc, nh, nx, hops, heads, tok, width,
    q_in, k_in, v_in, g_in, seg_in, fr_in,
    gq_out, gk_out, gv_out, wq_out,
    q, kv, g, seg, bias, fl, ff, flt, fft, sc, dp, dsb, pb,
    lbuf, rbuf, fbuf, acc, rs_s, rs_r, pks, pvs, pkr, pvr,
    in_sem, fl_sem, ff_sem, kv_s, kv_r, pp_s, pp_r, z_s, z_r, xl_s, xl_r, xf_s, xf_r, c_s, c_r,
):
    c = lax.axis_index("ctx")
    w = lax.axis_index("wide")
    x = lax.rem(w, nx)
    half = w // nx
    rows = width // nc
    nz = 2 * nh
    z = half * nh + lax.axis_index("head")
    part = tok // 2
    factor = HD ** (-0.5)

    def ctx(step):
        return {"ctx": lax.rem(c + step, nc)}

    def across(step):
        return {"wide": half * nx + lax.rem(x + step, nx)}

    def along(way):
        to = lax.rem(z + (1, -1)[way] * (nh // hops) + nz, nz)
        return {"head": lax.rem(to, nh), "wide": to // nh * nx + x}

    barrier = pltpu.get_barrier_semaphore()
    others = [along(0), along(1)] + [across(j) for j in range(1, nx)] + [ctx(j) for j in range(1, nc)]
    for other in others:
        pl.semaphore_signal(barrier, inc=1, device_id=other, device_id_type=MESH)

    loads = []
    for h in range(heads):
        cols = pl.ds(h * HD, HD)
        loads.append(pltpu.make_async_copy(q_in.at[0, :, cols], q.at[h], in_sem.at[4 * h]))
        loads.append(pltpu.make_async_copy(k_in.at[0, :, cols], kv.at[h, 0, pl.ds(tok, tok)], in_sem.at[4 * h + 1]))
        loads.append(pltpu.make_async_copy(g_in.at[0, :, cols], g.at[h], in_sem.at[4 * h + 2]))
        loads.append(pltpu.make_async_copy(v_in.at[0, :, cols], kv.at[h, 1, pl.ds(tok, tok)], in_sem.at[4 * h + 3]))
    loads.append(pltpu.make_async_copy(seg_in, seg.at[1], in_sem.at[4 * heads]))
    own_frames = pltpu.make_async_copy(fr_in.at[pl.ds(half * nx, nx)], fl, fl_sem)
    far_frames = pltpu.make_async_copy(fr_in.at[pl.ds((1 - half) * nx, nx)], ff, ff_sem)
    for copy in loads + [own_frames, far_frames]:
        copy.start()
    for copy in loads:
        copy.wait()

    @pl.when(c == 0)
    def _():
        seg[0] = jnp.zeros_like(seg[0])
        for h in range(heads):
            for n in range(2):
                kv[h, n, :tok] = jnp.zeros((tok, HD), BF16)

    @pl.when(c == nc - 1)
    def _():
        pkr[...] = jnp.zeros_like(pkr)
        pvr[...] = jnp.zeros_like(pvr)

    for h in range(heads):
        sc[h, :, tok:] = dot(q[h], kv[h, 0, tok:], ((1,), (1,))) * factor
        dp[h, :, tok:] = dot(g[h], kv[h, 1, tok:], ((1,), (1,)))


    pl.semaphore_wait(barrier, len(others))

    kv_copies = [
        remote(kv.at[h, :, pl.ds(tok, tok)], kv.at[h, :, pl.ds(0, tok)], kv_s.at[h], kv_r.at[h], ctx(1))
        for h in range(heads)
    ]
    seg_copy = remote(seg.at[1], seg.at[0], kv_s.at[heads], kv_r.at[heads], ctx(1))
    first = [seg_copy] + kv_copies
    has_prior, has_later = c > 0, c < nc - 1

    @pl.when(has_later)
    def _():
        for copy in first:
            copy.start()


    mine = jnp.broadcast_to(seg[1], (HD, tok)).T[:, :1]
    query_place = lax.broadcasted_iota(jnp.int32, (tok, tok), 0)
    key_place = lax.broadcasted_iota(jnp.int32, (tok, tok), 1)
    bias[:, tok:] = jnp.where((mine == seg[1]) & (key_place <= query_place), 0.0, LOW)
    pl.when(has_prior)(seg_copy.wait_recv)
    bias[:, :tok] = jnp.where((mine == seg[0]) & (c > 0), 0.0, LOW)

    z_copies = {}
    xl_copies = {}

    def hop(h, way, n, src):
        dst = fbuf.at[h, x, pl.ds(way * part, part)] if n == hops - 1 else rbuf.at[h, way, n]
        m = (2 * h + way) * hops + n
        copy = remote(src, dst, z_s.at[m], z_r.at[m], along(way))
        copy.start()
        z_copies[h, way, n] = copy

    for h in range(heads):
        pl.when(has_prior)(kv_copies[h].wait_recv)
        sc[h, :, :tok] = dot(q[h], kv[h, 0, :tok], ((1,), (1,))) * factor
        dp[h, :, :tok] = dot(g[h], kv[h, 1, :tok], ((1,), (1,)))
        scores = sc[h] + bias[...]
        row_max = jnp.max(scores, axis=1, keepdims=True)
        weight = jnp.exp(scores - row_max)
        prob = weight * (1.0 / jnp.sum(weight, axis=1, keepdims=True))
        grad_prob = dp[h]
        row_delta = jnp.sum(prob * grad_prob, axis=1, keepdims=True)
        grad_score = (prob * (grad_prob - row_delta)).astype(BF16)
        dsb[h] = grad_score
        pb[h] = prob.astype(BF16)
        grad_query = (dot(grad_score, kv[h, 0], ((1,), (0,))) * factor).astype(BF16)
        lbuf[h, x] = grad_query
        gq_out[0, :, h * HD : (h + 1) * HD] = grad_query
        for way in range(2):
            hop(h, way, 0, lbuf.at[h, x, pl.ds(way * part, part)])

    for j in range(1, nx):
        copy = remote(lbuf.at[:, x], lbuf.at[:, x], xl_s.at[j], xl_r.at[j], across(j))
        copy.start()
        xl_copies[j] = copy

    for h in range(heads):
        cols = slice(h * HD, (h + 1) * HD)
        pks[:, cols] = dot(dsb[h, :, :tok], q[h], ((0,), (0,)))
        pvs[:, cols] = dot(pb[h, :, :tok], g[h], ((0,), (0,)))
    pp = [
        remote(pks, pkr, pp_s.at[0], pp_r.at[0], ctx(nc - 1)),
        remote(pvs, pvr, pp_s.at[1], pp_r.at[1], ctx(nc - 1)),
    ]

    @pl.when(has_prior)
    def _():
        for copy in pp:
            copy.start()


    def near(h):
        total = dot(flt[0], lbuf[h, 0], ((1,), (0,)))
        for r in range(1, nx):
            total += dot(flt[r], lbuf[h, r], ((1,), (0,)))
        acc[h] = total

    def relay(n):
        for h in range(heads):
            for way in range(2):
                z_copies[h, way, n - 1].wait_recv()
                hop(h, way, n, rbuf.at[h, way, n - 1])

    relay(1)
    own_frames.wait()
    for r in range(nx):
        flt[r] = fl[r].T
    if hops > 2:
        relay(2)
    far_frames.wait()
    for r in range(nx):
        fft[r] = ff[r].T

    for n in range(3, hops):
        relay(n)

    for j in range(1, nx):
        xl_copies[j].wait_recv()
    for h in range(heads):
        near(h)

    @pl.when(has_later)
    def _():
        for copy in pp:
            copy.wait_recv()

    for h in range(heads):
        cols = slice(h * HD, (h + 1) * HD)
        own_key = dot(dsb[h, :, tok:], q[h], ((0,), (0,)))
        own_value = dot(pb[h, :, tok:], g[h], ((0,), (0,)))
        gk_out[0, :, cols] = ((own_key + pkr[:, cols]) * factor).astype(BF16)
        gv_out[0, :, cols] = (own_value + pvr[:, cols]).astype(BF16)

    xf_copies = {}
    c_copies = {}

    def pass_on(h):
        for way in range(2):
            z_copies[h, way, hops - 1].wait_recv()
        for j in range(1, nx):
            copy = remote(fbuf.at[h, x], fbuf.at[h, x], xf_s.at[h * nx + j], xf_r.at[h * nx + j], across(j))
            copy.start()
            xf_copies[h, j] = copy

    def add(h):
        total = acc[h] + dot(fft[x], fbuf[h, x], ((1,), (0,)))
        for j in range(1, nx):
            xf_copies[h, j].wait_recv()
            r = lax.rem(x - j + nx, nx)
            total += dot(fft[r], fbuf[h, r], ((1,), (0,)))
        acc[h] = total
        rs_s[h] = total.astype(BF16).reshape(nc, rows, HD)
        for j in range(1, nc):
            n = h * nc + j
            copy = remote(rs_s.at[h, lax.rem(c + j, nc)], rs_r.at[h, j], c_s.at[n], c_r.at[n], ctx(j))
            copy.start()
            c_copies[h, j] = copy

    for h in range(heads):
        pass_on(h)
    for h in range(heads):
        add(h)
    @pl.when(has_later)
    def _():
        for copy in first:
            copy.wait_send()

    @pl.when(has_prior)
    def _():
        for copy in pp:
            copy.wait_send()

    for group in (z_copies, xl_copies, xf_copies):
        for copy in group.values():
            copy.wait_send()

    own_rows = pl.ds(pl.multiple_of(c * rows, rows), rows)
    for h in range(heads):
        total = acc[h, own_rows]
        for j in range(1, nc):
            c_copies[h, j].wait_recv()
            total += rs_r[h, j].astype(F32)
        wq_out[0, :, h * HD : (h + 1) * HD] = total
    for copy in c_copies.values():
        copy.wait_send()


def store(*refs):
    n = len(refs) // 2
    for i in range(n):
        pltpu.make_async_copy(refs[i], refs[n + i], refs[-1].at[i]).start()
    for i in range(n):
        pltpu.make_async_copy(refs[i], refs[n + i], refs[-1].at[i]).wait()


def solution(mesh):
    nc, nh, nx = mesh.shape["ctx"], mesh.shape["head"], mesh.shape["wide"] // 2

    def shards(query_rows, key_rows, value_rows, grad_out, segment, frames):
        tok, columns = query_rows.shape[1:]
        heads = columns // HD
        width = frames.shape[2]
        rows = width // nc
        vm = pltpu.VMEM
        dma = pltpu.SemaphoreType.DMA
        shapes = [(1, tok, columns)] * 3 + [(1, rows, columns)]
        types = [BF16] * 3 + [F32]
        results = pl.pallas_call(
            functools.partial(kernel, nc, nh, nx, 4, heads, tok, width),
            name="attention_grads",
            out_shape=[vm(shape, kind) for shape, kind in zip(shapes, types)],
            in_specs=[pl.BlockSpec(memory_space=pl.ANY)] * 6,
            out_specs=[pl.BlockSpec(memory_space=vm)] * 4,
            scratch_shapes=[
                vm((heads, tok, HD), BF16),
                vm((heads, 2, 2 * tok, HD), BF16),
                vm((heads, tok, HD), BF16),
                vm((2, 1, tok), jnp.int32),
                vm((tok, 2 * tok), F32),
                vm((nx, tok, width), BF16),
                vm((nx, tok, width), BF16),
                vm((nx, width, tok), BF16),
                vm((nx, width, tok), BF16),
                vm((heads, tok, 2 * tok), F32),
                vm((heads, tok, 2 * tok), F32),
                vm((heads, tok, 2 * tok), BF16),
                vm((heads, tok, 2 * tok), BF16),
                vm((heads, nx, tok, HD), BF16),
                vm((heads, 2, 3, tok // 2, HD), BF16),
                vm((heads, nx, tok, HD), BF16),
                vm((heads, width, HD), F32),
                vm((heads, nc, rows, HD), BF16),
                vm((heads, nc, rows, HD), BF16),
                vm((tok, columns), F32),
                vm((tok, columns), F32),
                vm((tok, columns), F32),
                vm((tok, columns), F32),
                dma((4 * heads + 1,)),
                dma,
                dma,
                dma((heads + 1,)),
                dma((heads + 1,)),
                dma((2,)),
                dma((2,)),
                dma((heads * 8,)),
                dma((heads * 8,)),
                dma((nx,)),
                dma((nx,)),
                dma((heads * nx,)),
                dma((heads * nx,)),
                dma((heads * nc,)),
                dma((heads * nc,)),
            ],
            compiler_params=pltpu.CompilerParams(
                collective_id=0, has_side_effects=True, vmem_limit_bytes=60 * 1024 * 1024
            ),
        )(query_rows, key_rows, value_rows, grad_out, segment, frames)
        return pl.pallas_call(
            store,
            name="store",
            out_shape=[jax.ShapeDtypeStruct(shape, kind) for shape, kind in zip(shapes, types)],
            in_specs=[pl.BlockSpec(memory_space=pl.ANY)] * 4,
            out_specs=[pl.BlockSpec(memory_space=pl.ANY)] * 4,
            scratch_shapes=[dma((4,))],
            compiler_params=pltpu.CompilerParams(vmem_limit_bytes=1024 * 1024),
        )(*results)

    return jax.shard_map(
        shards,
        mesh=mesh,
        in_specs=(
            P("wide", "ctx", "head"),
            P("wide", "ctx", "head"),
            P("wide", "ctx", "head"),
            P("wide", "ctx", "head"),
            P("wide", "ctx"),
            P(None, "ctx", "wide"),
        ),
        out_specs=(
            P("wide", "ctx", "head"),
            P("wide", "ctx", "head"),
            P("wide", "ctx", "head"),
            P("wide", "ctx", "head"),
        ),
        check_vma=False,
    )
```
